256 devices in a mesh: group: 8 (over z_hi, x), ctx: 32 (over z_lo, y, core).
Axes of the slice: x: 4, y: 4, z: 8 (z_hi: 2, z_lo: 4; z = z_hi * 4 + z_lo), core: 2. Of those that a mesh axis runs over, the one named last changes fastest.
Arguments:
- queries: bfloat16 [65536, 4096], P(('group', 'ctx')), may hold values from -36 to 36
- resp_keys: bfloat16 [65536, 512], P(('group', 'ctx')), may hold values from -6 to 6
- resp_values: bfloat16 [65536, 512], P(('group', 'ctx')), may hold values from -6 to 6
- lengths: int32 [256], P(('group', 'ctx')), may hold values from 1 to 256, 49152 in all
- prefix_keys: bfloat16 [1024, 512], P(('group', 'ctx')), may hold values from -6 to 6
- prefix_values: bfloat16 [1024, 512], P(('group', 'ctx')), may hold values from -6 to 6
Outputs:
- attended: bfloat16 [65536, 4096], P(('group', 'ctx'))
The draws below stay inside these ranges and needn't reach their ends.
All inputs are finite; a program needn't handle non-finite values. No bound on the sum of `lengths` on one device may be relied on, other than what follows from the above.
Results may differ from the reference program's by a relative error of at most 0.0055.
Values may be sent and summed in bfloat16 or wider, within the bound.
A program may use at most 128 MiB of HBM per device.

```python
import math
import jax
import jax.numpy as jnp
import numpy as np
from jax import lax

HEADS = 32
KV_HEADS = 4
HEAD = 128
RLEN = 256
RESPONSES = 256
TOKENS = 65536
PREFIX = 1024


def draw_queries(key, part):
    key = jax.random.fold_in(key, 3)
    drawn = 2.0 * jax.random.truncated_normal(key, -6.0, 6.0, (TOKENS, HEADS, HEAD), jnp.float32)
    return drawn.reshape(TOKENS, HEADS * HEAD).astype(jnp.bfloat16)


def draw_prefix_keys(key, part):
    key = jax.random.fold_in(key, 5)
    drawn = jax.random.truncated_normal(key, -6.0, 6.0, (PREFIX, KV_HEADS, HEAD), jnp.float32)
    return drawn.reshape(PREFIX, KV_HEADS * HEAD).astype(jnp.bfloat16)


def levels(own_key, dims, cuts, least, high):
    def one(position, blocks):
        steps = jax.random.uniform(jax.random.fold_in(jax.random.fold_in(own_key, 6), position), (blocks,), jnp.float32, least / len(cuts), high / len(cuts))
        return jnp.repeat(jnp.exp(steps), dims[position] // blocks).reshape((-1,) + (1,) * (len(dims) - position - 1))

    level = one(*cuts[0])
    for cut in cuts[1:]:
        level = level * one(*cut)
    return level


def length_profile(count, total, reach, skew):
    loads = [(1 << 20) // math.isqrt(standing ** skew) + 1 for standing in range(2, count + 1)]
    surplus, holding = total - reach - (count - 1), [1] * (count - 1)
    while surplus > 0:
        candidates = [i for i in range(count - 1) if holding[i] < reach]
        pool, remaining = sum([loads[i] for i in candidates]), surplus
        for i in candidates:
            addition = min(reach - holding[i], max(1, remaining * loads[i] // pool), surplus)
            holding[i] = holding[i] + addition
            surplus = surplus - addition
    return np.array([reach] + holding)


def ragged(rng, amount, total, limit, lean):
    if amount == 2:
        one = jax.random.randint(rng, (), max(1, total - limit), min(limit, total - 1) + 1)
        return jnp.stack([one, total - one])
    sizes = jnp.asarray(length_profile(amount, total, limit, lean), jnp.int32)
    couples = (amount - 1) // 2
    source_of, receiver = sizes[1:1 + 2 * couples:2], sizes[2:2 + 2 * couples:2]
    room = jnp.minimum(source_of - 1, limit - receiver)
    moved = jax.random.randint(jax.random.fold_in(rng, 1), (couples,), 0, 1 << 20) % (room + 1)
    sizes = sizes.at[1:1 + 2 * couples:2].set(source_of - moved).at[2:2 + 2 * couples:2].set(receiver + moved)
    return sizes[jax.random.permutation(jax.random.fold_in(rng, 2), amount)]


def scatter_about(key, extent, width, bound, cuts=(), kind=jnp.bfloat16):
    factor_of = levels(key, extent, cuts, -0.22, 0.18) if cuts else 1.0
    values = jax.random.normal(key, extent, jnp.float32) * width * factor_of
    return jnp.minimum(jnp.maximum(values, -bound), bound).astype(kind)


def setup_inputs(seed: int = 0) -> dict:
    streams_of = jax.random.split(jax.random.key(seed), 7)
    queries = draw_queries(jax.random.fold_in(streams_of[6], 71), 0)
    resp_keys = scatter_about(streams_of[1], (TOKENS, KV_HEADS * HEAD), 1.0, 6.0, ((0, 256),))
    resp_values = scatter_about(streams_of[2], (TOKENS, KV_HEADS * HEAD), 1.0, 6.0, ((0, 256),))
    lengths = ragged(streams_of[3], RESPONSES, RESPONSES * RLEN * 3 // 4, RLEN, 0).astype(jnp.int32)
    prefix_keys = draw_prefix_keys(jax.random.fold_in(streams_of[6], 71), 0)
    prefix_values = scatter_about(streams_of[5], (PREFIX, KV_HEADS * HEAD), 1.0, 6.0, ((0, 256),))
    return {"queries": queries, "resp_keys": resp_keys, "resp_values": resp_values, "lengths": lengths, "prefix_keys": prefix_keys, "prefix_values": prefix_values}


def attend_one(query_rows, own_keys, own_values, live_count, prefix_keys, prefix_values):
    groups = HEADS // KV_HEADS
    grouped = query_rows.astype(jnp.float32).reshape(RLEN, KV_HEADS, groups, HEAD)
    key_rows = jnp.concatenate([own_keys, prefix_keys], axis=0).astype(jnp.float32).reshape(RLEN + PREFIX, KV_HEADS, HEAD)
    value_rows = jnp.concatenate([own_values, prefix_values], axis=0).astype(jnp.float32).reshape(RLEN + PREFIX, KV_HEADS, HEAD)
    scores = jnp.einsum('rkgd,nkd->rkgn', grouped, key_rows) * (1.0 / math.sqrt(HEAD))
    positions = jnp.arange(RLEN, dtype=jnp.int32)
    columns = jnp.arange(RLEN + PREFIX, dtype=jnp.int32)
    allowed = (columns[None, :] >= RLEN) | (columns[None, :] <= positions[:, None])
    scores = jnp.where(allowed[:, None, None, :], scores, -1e+30)
    row_max = lax.optimization_barrier(jnp.max(scores, axis=-1))
    weights = jnp.exp(scores - row_max[..., None])
    row_sum = lax.optimization_barrier(jnp.sum(weights, axis=-1))
    rounded = lax.optimization_barrier(weights.astype(jnp.bfloat16)).astype(jnp.float32)
    weighted = jnp.einsum('rkgn,nkd->rkgd', rounded, value_rows)
    result = weighted / row_sum[..., None]
    live_rows = positions < live_count
    result = jnp.where(live_rows[:, None, None, None], result, 0.0)
    return result.reshape(RLEN, HEADS * HEAD).astype(jnp.bfloat16)

def reference(queries, resp_keys, resp_values, lengths, prefix_keys, prefix_values):
    query_blocks = queries.reshape(RESPONSES, RLEN, HEADS * HEAD)
    key_blocks = resp_keys.reshape(RESPONSES, RLEN, KV_HEADS * HEAD)
    value_blocks = resp_values.reshape(RESPONSES, RLEN, KV_HEADS * HEAD)

    def one_response(packed):
        return attend_one(packed[0], packed[1], packed[2], packed[3], prefix_keys, prefix_values)
    outputs = lax.map(one_response, (query_blocks, key_blocks, value_blocks, lengths))
    return outputs.reshape(TOKENS, HEADS * HEAD)
```

```python
import math

import jax
import jax.numpy as jnp
from jax import lax
from jax.experimental import pallas as pl
from jax.experimental.pallas import tpu as pltpu
from jax.sharding import PartitionSpec as P

MESH = pl.DeviceIdType.MESH
KV_HEADS = 4
GROUPS = 8
HEAD = 128
ROWS = 256
BASE2_SCALE = math.log2(math.e) / math.sqrt(HEAD)
NT = (((1,), (1,)), ((), ()))
NN = (((1,), (0,)), ((), ()))

Z_OFFSETS = (0, 1, 7, 2, 6, 3, 5, 4)
PLANE_OFFSETS = sorted(
    [(a, b) for a in range(4) for b in range(4)],
    key=lambda ab: min(ab[0], 4 - ab[0]) + min(ab[1], 4 - ab[1]),
)
PLANES = len(Z_OFFSETS)
PEERS = len(PLANE_OFFSETS)

CHUNKS = ((0, 4), (4, 8))


def device(x, y, z, core):
    return ((z // 4) * 4 + x, (z % 4) * 8 + y * 2 + core)


def matmul(a, b, dims):
    return lax.dot_general(a, b, dims, preferred_element_type=jnp.float32)


def head_lanes(index):
    return pl.ds(pl.multiple_of(index * HEAD, HEAD), HEAD)


def attend(h, keys, values, first, last, live, q_ref, out_ref, acc_ref, max_ref):
    ones = jnp.ones((values.shape[0], HEAD), jnp.bfloat16)
    values_and_ones = jnp.concatenate([values, ones], axis=1)

    def scores_of(g):
        return matmul(q_ref[:, head_lanes(h * GROUPS + g)], keys, NT)

    def weigh(g, scores):
        head = h * GROUPS + g
        if first:
            own = keys.shape[0]
            column = lax.broadcasted_iota(jnp.int32, (ROWS, own), 1)
            row = lax.broadcasted_iota(jnp.int32, (ROWS, own), 0)
            scores = jnp.where(column <= row, scores, -1e30)
        top = jnp.max(scores, axis=1, keepdims=True) * BASE2_SCALE
        top = jnp.broadcast_to(top, (ROWS, HEAD))
        factor = None
        if not first:
            before = max_ref[head]
            top = jnp.maximum(before, top)
            factor = jnp.exp2(before - top)
        if not last:
            max_ref[head] = top
        parts = [
            jnp.exp2(scores[:, i : i + HEAD] * BASE2_SCALE - top).astype(jnp.bfloat16)
            for i in range(0, scores.shape[1], HEAD)
        ]
        return jnp.concatenate(parts, axis=1), factor

    def mix(g, weights, factor):
        head = h * GROUPS + g
        total = matmul(weights, values_and_ones, NN)
        if not first:
            total = acc_ref[head] * jnp.concatenate([factor, factor], axis=1) + total
        if not last:
            acc_ref[head] = total
            return
        result = total[:, :HEAD] * (1.0 / total[:, HEAD:])
        position = lax.broadcasted_iota(jnp.int32, (ROWS, HEAD), 0)
        result = jnp.where(position < live, result, 0.0)
        out_ref[:, head_lanes(head)] = result.astype(jnp.bfloat16)

    following = scores_of(0)
    for g in range(GROUPS):
        current = following
        if g + 1 < GROUPS:
            following = scores_of(g + 1)
        mix(g, *weigh(g, current))


def kernel(
    q_hbm, ok_hbm, ov_hbm, len_ref, pk_hbm, pv_hbm, out_hbm,
    q_ref, ok_ref, ov_ref, pk_ref, pv_ref, out_ref, acc_ref, max_ref, plane_ref, kv_ref,
    load_sems, store_sems, z_send, z_recv, plane_send, plane_recv, core_send, core_recv,
):
    group, ctx = lax.axis_index("group"), lax.axis_index("ctx")
    x, z = group % 4, (group // 4) * 4 + ctx // 8
    y, core = (ctx // 2) % 4, ctx % 2
    plane_peers = [device((x + a) % 4, (y + b) % 4, z, core) for a, b in PLANE_OFFSETS]
    z_peers = [device(x, y, (z + off) % 8, core) for off in Z_OFFSETS]
    sibling = device(x, y, z, 1 - core)

    barrier = pltpu.get_barrier_semaphore()
    for peer in plane_peers[1:] + z_peers[1:] + [sibling]:
        pl.semaphore_signal(barrier, inc=1, device_id=peer, device_id_type=MESH)

    loads = [
        pltpu.make_async_copy(src, dst, load_sems.at[i])
        for i, (src, dst) in enumerate(
            [(pk_hbm, pk_ref), (pv_hbm, pv_ref), (ok_hbm, ok_ref), (ov_hbm, ov_ref), (q_hbm, q_ref)]
        )
    ]
    for load in loads:
        load.start()
    loads[0].wait()
    loads[1].wait()
    for h in range(KV_HEADS):
        rows, lanes = slice(4 * h, 4 * h + 4), slice(HEAD * h, HEAD * h + HEAD)
        plane_ref[0, 0, 0, rows] = pk_ref[:, lanes]
        plane_ref[0, 0, 1, rows] = pv_ref[:, lanes]

    def remote(src, dst, send_sem, recv_sem, peer):
        return pltpu.make_async_remote_copy(
            src_ref=src, dst_ref=dst, send_sem=send_sem, recv_sem=recv_sem,
            device_id=peer, device_id_type=MESH,
        )

    z_copies = [
        remote(plane_ref.at[0, 0], plane_ref.at[j, 0], z_send.at[j], z_recv.at[j], z_peers[j])
        for j in range(1, PLANES)
    ]

    def send_plane(j):
        for p in range(1, PEERS):
            remote(
                plane_ref.at[j, 0], plane_ref.at[j, p],
                plane_send.at[j], plane_recv.at[j], plane_peers[p],
            ).start()

    def wait_plane(j, sems):
        whole = plane_ref.at[j, pl.ds(1, PEERS - 1)]
        pltpu.make_async_copy(whole, whole, sems.at[j]).wait()

    def core_copy(j):
        return remote(kv_ref.at[j, 0], kv_ref.at[j, 1], core_send.at[j], core_recv.at[j], sibling)

    def share_plane(j):
        wait_plane(j, plane_recv)
        for i in range(2):
            for a in range(4):
                for h in range(KV_HEADS):
                    kv_ref[j, 0, i, 16 * a : 16 * a + 16, HEAD * h : HEAD * h + HEAD] = jnp.concatenate(
                        [plane_ref[j, 4 * a + b, i, 4 * h : 4 * h + 4] for b in range(4)], axis=0
                    )
        core_copy(j).start()

    live = len_ref[0]
    refs = (live, q_ref, out_ref, acc_ref, max_ref)

    def own(h, carry):
        lanes = head_lanes(h)
        attend(h, ok_ref[:, lanes], ov_ref[:, lanes], True, False, *refs)
        return carry

    pl.semaphore_wait(barrier, PEERS - 1 + PLANES - 1 + 1)
    for copy in z_copies:
        copy.start()
    send_plane(0)
    for load in loads[2:]:
        load.wait()
    lax.fori_loop(0, 3, own, 0)
    for j in (1, 2):
        z_copies[j - 1].wait_recv()
        send_plane(j)
    lax.fori_loop(3, 4, own, 0)
    for j in range(3, PLANES):
        z_copies[j - 1].wait_recv()
        send_plane(j)

    for j in range(*CHUNKS[0]):
        share_plane(j)
    for index, (begin, end) in enumerate(CHUNKS):
        last = index + 1 == len(CHUNKS)
        for j in range(begin, end):
            core_copy(j).wait_recv()

        def prompt(h, carry, begin=begin, end=end, last=last):
            lanes = head_lanes(h)
            count = (end - begin) * 128
            keys = kv_ref[begin:end, :, 0, :, lanes].reshape(count, HEAD)
            values = kv_ref[begin:end, :, 1, :, lanes].reshape(count, HEAD)
            attend(h, keys, values, False, last, *refs)
            if last:
                columns = pl.ds(pl.multiple_of(h * GROUPS * HEAD, GROUPS * HEAD), GROUPS * HEAD)
                pltpu.make_async_copy(
                    out_ref.at[:, columns], out_hbm.at[:, columns], store_sems.at[h]
                ).start()
            else:
                share_plane(end + h)
            return carry

        lax.fori_loop(0, KV_HEADS, prompt, 0)

    for copy in z_copies:
        copy.wait_send()
    for j in range(PLANES):
        wait_plane(j, plane_send)
        core_copy(j).wait_send()
    for h in range(KV_HEADS):
        columns = pl.ds(h * GROUPS * HEAD, GROUPS * HEAD)
        pltpu.make_async_copy(
            out_ref.at[:, columns], out_hbm.at[:, columns], store_sems.at[h]
        ).wait()


def shards(queries, resp_keys, resp_values, lengths, prefix_keys, prefix_values):
    hbm = pl.BlockSpec(memory_space=pl.ANY)
    bf16, f32 = jnp.bfloat16, jnp.float32
    heads = KV_HEADS * GROUPS
    return pl.pallas_call(
        kernel,
        out_shape=jax.ShapeDtypeStruct(queries.shape, bf16),
        in_specs=[hbm, hbm, hbm, pl.BlockSpec(memory_space=pltpu.SMEM), hbm, hbm],
        out_specs=hbm,
        scratch_shapes=[
            pltpu.VMEM(queries.shape, bf16),
            pltpu.VMEM(resp_keys.shape, bf16),
            pltpu.VMEM(resp_values.shape, bf16),
            pltpu.VMEM(prefix_keys.shape, bf16),
            pltpu.VMEM(prefix_values.shape, bf16),
            pltpu.VMEM(queries.shape, bf16),
            pltpu.VMEM((heads, ROWS, 2 * HEAD), f32),
            pltpu.VMEM((heads, ROWS, HEAD), f32),
            pltpu.VMEM((PLANES, PEERS, 2, 16, HEAD), bf16),
            pltpu.VMEM((PLANES, 2, 2, 64, KV_HEADS * HEAD), bf16),
            pltpu.SemaphoreType.DMA((5,)),
            pltpu.SemaphoreType.DMA((KV_HEADS,)),
        ]
        + [pltpu.SemaphoreType.DMA((PLANES,))] * 6,
        compiler_params=pltpu.CompilerParams(
            collective_id=0, has_side_effects=True, vmem_limit_bytes=48 << 20
        ),
        name="attend_and_gather",
    )(queries, resp_keys, resp_values, lengths, prefix_keys, prefix_values)


def solution(mesh):
    rows = P(("group", "ctx"), None)
    in_specs = (rows, rows, rows, P(("group", "ctx")), rows, rows)
    return jax.shard_map(shards, mesh=mesh, in_specs=in_specs, out_specs=rows, check_vma=False)
```

```python
import math

import jax
import jax.numpy as jnp
from jax import lax
from jax.experimental import pallas as pl
from jax.experimental.pallas import tpu as pltpu
from jax.sharding import PartitionSpec as P

MESH = pl.DeviceIdType.MESH
KV_HEADS = 4
GROUPS = 8
HEAD = 128
ROWS = 256
BASE2_SCALE = math.log2(math.e) / math.sqrt(HEAD)
NT = (((1,), (1,)), ((), ()))
NN = (((1,), (0,)), ((), ()))

Z_OFFSETS = (0, 1, 7, 2, 6, 3, 5, 4)
RING_OFFSETS = (0, 1, 3, 2)
PLANES = len(Z_OFFSETS)
RING = len(RING_OFFSETS)

CHUNKS = ((0, 2), (2, 8))


def device(x, y, z, core):
    return ((z // 4) * 4 + x, (z % 4) * 8 + y * 2 + core)


def matmul(a, b, dims):
    return lax.dot_general(a, b, dims, preferred_element_type=jnp.float32)


def head_lanes(index):
    return pl.ds(pl.multiple_of(index * HEAD, HEAD), HEAD)


def attend(h, keys, values, first, last, len_ref, q_ref, out_ref, acc_ref, max_ref):
    ones = jnp.ones((values.shape[0], HEAD), jnp.bfloat16)
    values_and_ones = jnp.concatenate([values, ones], axis=1)

    def scores_of(g):
        return matmul(q_ref[:, head_lanes(h * GROUPS + g)], keys, NT)

    def weigh(g, scores):
        head = h * GROUPS + g
        if first:
            own = keys.shape[0]
            column = lax.broadcasted_iota(jnp.int32, (ROWS, own), 1)
            row = lax.broadcasted_iota(jnp.int32, (ROWS, own), 0)
            scores = jnp.where(column <= row, scores, -1e30)
        top = jnp.max(scores, axis=1, keepdims=True) * BASE2_SCALE
        top = jnp.broadcast_to(top, (ROWS, HEAD))
        factor = None
        if not first:
            before = max_ref[head]
            top = jnp.maximum(before, top)
            factor = jnp.exp2(before - top)
        if not last:
            max_ref[head] = top
        parts = [
            jnp.exp2(scores[:, i : i + HEAD] * BASE2_SCALE - top).astype(jnp.bfloat16)
            for i in range(0, scores.shape[1], HEAD)
        ]
        return jnp.concatenate(parts, axis=1), factor

    def mix(g, weights, factor):
        head = h * GROUPS + g
        total = matmul(weights, values_and_ones, NN)
        if not first:
            total = acc_ref[head] * jnp.concatenate([factor, factor], axis=1) + total
        if not last:
            acc_ref[head] = total
            return
        result = total[:, :HEAD] * (1.0 / total[:, HEAD:])
        position = lax.broadcasted_iota(jnp.int32, (ROWS, HEAD), 0)
        result = jnp.where(position < len_ref[0], result, 0.0)
        out_ref[:, head_lanes(head)] = result.astype(jnp.bfloat16)

    following = scores_of(0)
    for g in range(GROUPS):
        current = following
        if g + 1 < GROUPS:
            following = scores_of(g + 1)
        mix(g, *weigh(g, current))


def kernel(
    q_hbm, ok_hbm, ov_hbm, len_hbm, pk_hbm, pv_hbm, out_hbm,
    len_ref, q_ref, ok_ref, ov_ref, pk_ref, pv_ref, out_ref, acc_ref, max_ref, part_ref, kv_ref,
    load_sems, store_sems, part_send, part_recv, plane_send, plane_recv, core_send, core_recv,
):
    group, ctx = lax.axis_index("group"), lax.axis_index("ctx")
    x, z = group % 4, (group // 4) * 4 + ctx // 8
    y, core = (ctx // 2) % 4, ctx % 2

    def first_peer(a, j):
        return device(
            (x + RING_OFFSETS[a] * (1 - core)) % 4,
            (y + RING_OFFSETS[a] * core) % 4,
            (z + Z_OFFSETS[j]) % 8,
            core,
        )

    def last_peer(b):
        return device(
            (x + RING_OFFSETS[b] * core) % 4, (y + RING_OFFSETS[b] * (1 - core)) % 4, z, core
        )

    sibling = device(x, y, z, 1 - core)
    first_peers = {(a, j): first_peer(a, j) for j in range(PLANES) for a in range(RING) if a + j}
    last_peers = [last_peer(b) for b in range(RING)]

    barrier = pltpu.get_barrier_semaphore()
    for peer in list(first_peers.values()) + last_peers[1:] + [sibling]:
        pl.semaphore_signal(barrier, inc=1, device_id=peer, device_id_type=MESH)

    loads = [
        pltpu.make_async_copy(src, dst, load_sems.at[i])
        for i, (src, dst) in enumerate(
            [
                (pk_hbm, pk_ref), (pv_hbm, pv_ref), (len_hbm, len_ref),
                (ok_hbm, ok_ref), (ov_hbm, ov_ref), (q_hbm, q_ref),
            ]
        )
    ]
    for load in loads:
        load.start()
    loads[0].wait()
    loads[1].wait()
    for h in range(KV_HEADS):
        rows, lanes = slice(4 * h, 4 * h + 4), slice(HEAD * h, HEAD * h + HEAD)
        part_ref[0, 0, 0, rows] = pk_ref[:, lanes]
        part_ref[0, 0, 1, rows] = pv_ref[:, lanes]

    def remote(src, dst, send_sem, recv_sem, peer):
        return pltpu.make_async_remote_copy(
            src_ref=src, dst_ref=dst, send_sem=send_sem, recv_sem=recv_sem,
            device_id=peer, device_id_type=MESH,
        )

    def send_part():
        for j in range(PLANES):
            for a in range(RING):
                if a + j:
                    remote(
                        part_ref.at[0, 0], part_ref.at[j, a],
                        part_send.at[j], part_recv.at[j], first_peers[a, j],
                    ).start()

    def wait_part(j, sems):
        whole = part_ref.at[j] if j else part_ref.at[0, pl.ds(1, RING - 1)]
        pltpu.make_async_copy(whole, whole, sems.at[j]).wait()

    def send_plane(j):
        wait_part(j, part_recv)
        for i in range(2):
            for h in range(KV_HEADS):
                kv_ref[j, 0, 0, i, :, HEAD * h : HEAD * h + HEAD] = jnp.concatenate(
                    [part_ref[j, a, i, 4 * h : 4 * h + 4] for a in range(RING)], axis=0
                )
        for b in range(1, RING):
            remote(
                kv_ref.at[j, 0, 0], kv_ref.at[j, 0, b],
                plane_send.at[j], plane_recv.at[j], last_peers[b],
            ).start()

    def wait_plane(j, sems):
        whole = kv_ref.at[j, 0, pl.ds(1, RING - 1)]
        pltpu.make_async_copy(whole, whole, sems.at[j]).wait()

    def core_copy(j):
        return remote(kv_ref.at[j, 0], kv_ref.at[j, 1], core_send.at[j], core_recv.at[j], sibling)

    def share_plane(j):
        wait_plane(j, plane_recv)
        core_copy(j).start()

    refs = (len_ref, q_ref, out_ref, acc_ref, max_ref)

    def own(h, carry):
        lanes = head_lanes(h)
        attend(h, ok_ref[:, lanes], ov_ref[:, lanes], True, False, *refs)
        return carry

    pl.semaphore_wait(barrier, len(first_peers) + RING - 1 + 1)
    send_part()
    for load in loads[2:]:
        load.wait()
    lax.fori_loop(0, KV_HEADS, own, 0)
    shared = 0
    for j in range(PLANES):
        send_plane(j)
        if j >= 2 and j % 2 == 0 and shared < CHUNKS[0][1]:
            share_plane(shared)
            shared += 1
    for j in range(shared, CHUNKS[0][1]):
        share_plane(j)
    for index, (begin, end) in enumerate(CHUNKS):
        last = index + 1 == len(CHUNKS)
        coming = 0 if last else CHUNKS[index + 1][1] - end
        for j in range(begin, end):
            core_copy(j).wait_recv()

        def prompt(h, carry, begin=begin, end=end, last=last, coming=coming):
            lanes = head_lanes(h)
            count = (end - begin) * 128
            keys = kv_ref[begin:end, :, :, 0, :, lanes].reshape(count, HEAD)
            values = kv_ref[begin:end, :, :, 1, :, lanes].reshape(count, HEAD)
            attend(h, keys, values, False, last, *refs)
            if last:
                columns = pl.ds(pl.multiple_of(h * GROUPS * HEAD, GROUPS * HEAD), GROUPS * HEAD)
                pltpu.make_async_copy(
                    out_ref.at[:, columns], out_hbm.at[:, columns], store_sems.at[h]
                ).start()
            elif coming >= KV_HEADS:
                share_plane(end + h)
            else:

                @pl.when(h < coming)
                def _():
                    share_plane(end + h)

            return carry

        lax.fori_loop(0, KV_HEADS, prompt, 0)
        for j in range(end + KV_HEADS, end + coming):
            share_plane(j)

    for j in range(PLANES):
        wait_part(j, part_send)
        wait_plane(j, plane_send)
        core_copy(j).wait_send()
    for h in range(KV_HEADS):
        columns = pl.ds(h * GROUPS * HEAD, GROUPS * HEAD)
        pltpu.make_async_copy(
            out_ref.at[:, columns], out_hbm.at[:, columns], store_sems.at[h]
        ).wait()


def shards(queries, resp_keys, resp_values, lengths, prefix_keys, prefix_values):
    hbm = pl.BlockSpec(memory_space=pl.ANY)
    bf16, f32 = jnp.bfloat16, jnp.float32
    heads = KV_HEADS * GROUPS
    return pl.pallas_call(
        kernel,
        out_shape=pltpu.VMEM(queries.shape, bf16),
        in_specs=[hbm] * 6,
        out_specs=hbm,
        scratch_shapes=[
            pltpu.SMEM(lengths.shape, jnp.int32),
            pltpu.VMEM(queries.shape, bf16),
            pltpu.VMEM(resp_keys.shape, bf16),
            pltpu.VMEM(resp_values.shape, bf16),
            pltpu.VMEM(prefix_keys.shape, bf16),
            pltpu.VMEM(prefix_values.shape, bf16),
            pltpu.VMEM(queries.shape, bf16),
            pltpu.VMEM((heads, ROWS, 2 * HEAD), f32),
            pltpu.VMEM((heads, ROWS, HEAD), f32),
            pltpu.VMEM((PLANES, RING, 2, 16, HEAD), bf16),
            pltpu.VMEM((PLANES, 2, RING, 2, 16, KV_HEADS * HEAD), bf16),
            pltpu.SemaphoreType.DMA((6,)),
            pltpu.SemaphoreType.DMA((KV_HEADS,)),
        ]
        + [pltpu.SemaphoreType.DMA((PLANES,))] * 6,
        compiler_params=pltpu.CompilerParams(
            collective_id=0, has_side_effects=True, vmem_limit_bytes=58 << 20
        ),
        name="attend_and_gather",
    )(queries, resp_keys, resp_values, lengths, prefix_keys, prefix_values)


def solution(mesh):
    rows = P(("group", "ctx"), None)
    in_specs = (rows, rows, rows, P(("group", "ctx")), rows, rows)
    return jax.shard_map(shards, mesh=mesh, in_specs=in_specs, out_specs=rows, check_vma=False)
```

```python
import math

import jax
import jax.numpy as jnp
from jax import lax
from jax.experimental import pallas as pl
from jax.experimental.pallas import tpu as pltpu
from jax.sharding import PartitionSpec as P

MESH = pl.DeviceIdType.MESH
KV_HEADS = 4
GROUPS = 8
HEAD = 128
ROWS = 256
BASE2_SCALE = math.log2(math.e) / math.sqrt(HEAD)
NT = (((1,), (1,)), ((), ()))
NN = (((1,), (0,)), ((), ()))

Z_OFFSETS = (0, 1, 7, 2, 6, 3, 5, 4)
RING_OFFSETS = (0, 1, 3, 2)
PLANES = len(Z_OFFSETS)
RING = len(RING_OFFSETS)

CHUNKS = ((0, 2), (2, 8))


def device(x, y, z, core):
    return ((z // 4) * 4 + x, (z % 4) * 8 + y * 2 + core)


def matmul(a, b, dims):
    return lax.dot_general(a, b, dims, preferred_element_type=jnp.float32)


def head_lanes(index):
    return pl.ds(pl.multiple_of(index * HEAD, HEAD), HEAD)


def attend(h, keys, values, first, last, len_ref, q_ref, out_ref, acc_ref, max_ref):
    ones = jnp.ones((values.shape[0], HEAD), jnp.bfloat16)
    values_and_ones = jnp.concatenate([values, ones], axis=1)

    def scores_of(g):
        return matmul(q_ref[:, head_lanes(h * GROUPS + g)], keys, NT)

    def weigh(g, scores):
        head = h * GROUPS + g
        if first:
            own = keys.shape[0]
            column = lax.broadcasted_iota(jnp.int32, (ROWS, own), 1)
            row = lax.broadcasted_iota(jnp.int32, (ROWS, own), 0)
            scores = jnp.where(column <= row, scores, -1e30)
        top = jnp.max(scores, axis=1, keepdims=True) * BASE2_SCALE
        top = jnp.broadcast_to(top, (ROWS, HEAD))
        factor = None
        if not first:
            before = max_ref[head]
            top = jnp.maximum(before, top)
            factor = jnp.exp2(before - top)
        if not last:
            max_ref[head] = top
        parts = [
            jnp.exp2(scores[:, i : i + HEAD] * BASE2_SCALE - top).astype(jnp.bfloat16)
            for i in range(0, scores.shape[1], HEAD)
        ]
        return jnp.concatenate(parts, axis=1), factor

    def mix(g, weights, factor):
        head = h * GROUPS + g
        total = matmul(weights, values_and_ones, NN)
        if not first:
            total = acc_ref[head] * jnp.concatenate([factor, factor], axis=1) + total
        if not last:
            acc_ref[head] = total
            return
        result = total[:, :HEAD] * (1.0 / total[:, HEAD:])
        position = lax.broadcasted_iota(jnp.int32, (ROWS, HEAD), 0)
        result = jnp.where(position < len_ref[0], result, 0.0)
        out_ref[:, head_lanes(head)] = result.astype(jnp.bfloat16)

    following = scores_of(0)
    for g in range(GROUPS):
        current = following
        if g + 1 < GROUPS:
            following = scores_of(g + 1)
        mix(g, *weigh(g, current))


def kernel(
    q_hbm, ok_hbm, ov_hbm, len_hbm, pk_hbm, pv_hbm, out_ref,
    len_ref, q_ref, ok_ref, ov_ref, pk_ref, pv_ref, acc_ref, max_ref, part_ref, kv_ref,
    load_sems, part_send, part_recv, plane_send, plane_recv, core_send, core_recv,
):
    group, ctx = lax.axis_index("group"), lax.axis_index("ctx")
    x, z = group % 4, (group // 4) * 4 + ctx // 8
    y, core = (ctx // 2) % 4, ctx % 2

    def first_peer(a, j):
        return device(
            (x + RING_OFFSETS[a] * (1 - core)) % 4,
            (y + RING_OFFSETS[a] * core) % 4,
            (z + Z_OFFSETS[j]) % 8,
            core,
        )

    def last_peer(b):
        return device(
            (x + RING_OFFSETS[b] * core) % 4, (y + RING_OFFSETS[b] * (1 - core)) % 4, z, core
        )

    sibling = device(x, y, z, 1 - core)
    first_peers = {(a, j): first_peer(a, j) for j in range(PLANES) for a in range(RING) if a + j}
    last_peers = [last_peer(b) for b in range(RING)]

    barrier = pltpu.get_barrier_semaphore()
    for peer in list(first_peers.values()) + last_peers[1:] + [sibling]:
        pl.semaphore_signal(barrier, inc=1, device_id=peer, device_id_type=MESH)

    loads = [
        pltpu.make_async_copy(src, dst, load_sems.at[i])
        for i, (src, dst) in enumerate(
            [
                (pk_hbm, pk_ref), (pv_hbm, pv_ref), (len_hbm, len_ref),
                (ok_hbm, ok_ref), (ov_hbm, ov_ref), (q_hbm, q_ref),
            ]
        )
    ]
    for load in loads:
        load.start()
    loads[0].wait()
    loads[1].wait()
    for h in range(KV_HEADS):
        rows, lanes = slice(4 * h, 4 * h + 4), slice(HEAD * h, HEAD * h + HEAD)
        part_ref[0, 0, 0, rows] = pk_ref[:, lanes]
        part_ref[0, 0, 1, rows] = pv_ref[:, lanes]

    def remote(src, dst, send_sem, recv_sem, peer):
        return pltpu.make_async_remote_copy(
            src_ref=src, dst_ref=dst, send_sem=send_sem, recv_sem=recv_sem,
            device_id=peer, device_id_type=MESH,
        )

    def send_part():
        for j in range(PLANES):
            for a in range(RING):
                if a + j:
                    remote(
                        part_ref.at[0, 0], part_ref.at[j, a],
                        part_send.at[j], part_recv.at[j], first_peers[a, j],
                    ).start()

    def wait_part(j, sems):
        whole = part_ref.at[j] if j else part_ref.at[0, pl.ds(1, RING - 1)]
        pltpu.make_async_copy(whole, whole, sems.at[j]).wait()

    def send_plane(j):
        wait_part(j, part_recv)
        for i in range(2):
            for h in range(KV_HEADS):
                kv_ref[j, 0, 0, i, :, HEAD * h : HEAD * h + HEAD] = jnp.concatenate(
                    [part_ref[j, a, i, 4 * h : 4 * h + 4] for a in range(RING)], axis=0
                )
        for b in range(1, RING):
            remote(
                kv_ref.at[j, 0, 0], kv_ref.at[j, 0, b],
                plane_send.at[j], plane_recv.at[j], last_peers[b],
            ).start()

    def wait_plane(j, sems):
        whole = kv_ref.at[j, 0, pl.ds(1, RING - 1)]
        pltpu.make_async_copy(whole, whole, sems.at[j]).wait()

    def core_copy(j):
        return remote(kv_ref.at[j, 0], kv_ref.at[j, 1], core_send.at[j], core_recv.at[j], sibling)

    def share_plane(j):
        wait_plane(j, plane_recv)
        core_copy(j).start()

    refs = (len_ref, q_ref, out_ref, acc_ref, max_ref)

    def own(h, carry):
        lanes = head_lanes(h)
        attend(h, ok_ref[:, lanes], ov_ref[:, lanes], True, False, *refs)
        return carry

    pl.semaphore_wait(barrier, len(first_peers) + RING - 1 + 1)
    send_part()
    for load in loads[2:]:
        load.wait()
    lax.fori_loop(0, KV_HEADS - 1, own, 0)
    shared = 0
    for j in range(PLANES):
        if j == 1:
            lax.fori_loop(KV_HEADS - 1, KV_HEADS, own, 0)
        send_plane(j)
        if j >= 2 and j % 2 == 0 and shared < CHUNKS[0][1]:
            share_plane(shared)
            shared += 1
    for j in range(shared, CHUNKS[0][1]):
        share_plane(j)
    for index, (begin, end) in enumerate(CHUNKS):
        last = index + 1 == len(CHUNKS)
        coming = 0 if last else CHUNKS[index + 1][1] - end
        for j in range(begin, end):
            core_copy(j).wait_recv()

        def prompt(h, carry, begin=begin, end=end, last=last, coming=coming):
            lanes = head_lanes(h)
            count = (end - begin) * 128
            keys = kv_ref[begin:end, :, :, 0, :, lanes].reshape(count, HEAD)
            values = kv_ref[begin:end, :, :, 1, :, lanes].reshape(count, HEAD)
            attend(h, keys, values, False, last, *refs)
            if coming >= KV_HEADS:

                @pl.when(h == 1)
                def _():
                    share_plane(end)
                    share_plane(end + 1)

                @pl.when(h == 2)
                def _():
                    share_plane(end + 2)
                    share_plane(end + 3)
            elif coming:

                @pl.when(h < coming)
                def _():
                    share_plane(end + h)

            return carry

        lax.fori_loop(0, KV_HEADS, prompt, 0)
        for j in range(end + KV_HEADS, end + coming):
            share_plane(j)

    for j in range(PLANES):
        wait_part(j, part_send)
        wait_plane(j, plane_send)
        core_copy(j).wait_send()


def shards(queries, resp_keys, resp_values, lengths, prefix_keys, prefix_values):
    hbm = pl.BlockSpec(memory_space=pl.ANY)
    bf16, f32 = jnp.bfloat16, jnp.float32
    heads = KV_HEADS * GROUPS
    return pl.pallas_call(
        kernel,
        out_shape=pltpu.VMEM(queries.shape, bf16),
        in_specs=[hbm] * 6,
        out_specs=pl.BlockSpec(memory_space=pltpu.VMEM),
        scratch_shapes=[
            pltpu.SMEM(lengths.shape, jnp.int32),
            pltpu.VMEM(queries.shape, bf16),
            pltpu.VMEM(resp_keys.shape, bf16),
            pltpu.VMEM(resp_values.shape, bf16),
            pltpu.VMEM(prefix_keys.shape, bf16),
            pltpu.VMEM(prefix_values.shape, bf16),
            pltpu.VMEM((heads, ROWS, 2 * HEAD), f32),
            pltpu.VMEM((heads, ROWS, HEAD), f32),
            pltpu.VMEM((PLANES, RING, 2, 16, HEAD), bf16),
            pltpu.VMEM((PLANES, 2, RING, 2, 16, KV_HEADS * HEAD), bf16),
            pltpu.SemaphoreType.DMA((6,)),
        ]
        + [pltpu.SemaphoreType.DMA((PLANES,))] * 6,
        compiler_params=pltpu.CompilerParams(
            collective_id=0, has_side_effects=True, vmem_limit_bytes=58 << 20
        ),
        name="attend_and_gather",
    )(queries, resp_keys, resp_values, lengths, prefix_keys, prefix_values)


def solution(mesh):
    rows = P(("group", "ctx"), None)
    in_specs = (rows, rows, rows, P(("group", "ctx")), rows, rows)
    return jax.shard_map(shards, mesh=mesh, in_specs=in_specs, out_specs=rows, check_vma=False)
```

```python
import math

import jax
import jax.numpy as jnp
from jax import lax
from jax.experimental import pallas as pl
from jax.experimental.pallas import tpu as pltpu
from jax.sharding import PartitionSpec as P

MESH = pl.DeviceIdType.MESH
KV_HEADS = 4
GROUPS = 8
HEAD = 128
ROWS = 256
BASE2_SCALE = math.log2(math.e) / math.sqrt(HEAD)
NT = (((1,), (1,)), ((), ()))
NN = (((1,), (0,)), ((), ()))

Z_OFFSETS = (0, 1, 7, 2, 6, 3, 5, 4)
RING_OFFSETS = (0, 1, 3, 2)
PLANES = len(Z_OFFSETS)
RING = len(RING_OFFSETS)

CHUNKS = ((0, 2), (2, 8))
LAST_HEADS = 2


def device(x, y, z, core):
    return ((z // 4) * 4 + x, (z % 4) * 8 + y * 2 + core)


def matmul(a, b, dims):
    return lax.dot_general(a, b, dims, preferred_element_type=jnp.float32)


def head_lanes(index):
    return pl.ds(pl.multiple_of(index * HEAD, HEAD), HEAD)


def attend(blocks, first, last, len_ref, q_ref, out_ref, acc_ref, max_ref):
    count = blocks[0][1].shape[0]
    ones = jnp.ones((count, HEAD), jnp.bfloat16)
    heads = [(h * GROUPS + g, n) for n, (h, _, _) in enumerate(blocks) for g in range(GROUPS)]

    def scores_of(head, n):
        return matmul(q_ref[:, head_lanes(head)], blocks[n][1], NT)

    def weigh(head, scores):
        if first:
            column = lax.broadcasted_iota(jnp.int32, (ROWS, count), 1)
            row = lax.broadcasted_iota(jnp.int32, (ROWS, count), 0)
            scores = jnp.where(column <= row, scores, -1e30)
        top = jnp.max(scores, axis=1, keepdims=True) * BASE2_SCALE
        top = jnp.broadcast_to(top, (ROWS, HEAD))
        factor = None
        if not first:
            before = max_ref[head]
            top = jnp.maximum(before, top)
            factor = jnp.exp2(before - top)
        if not last:
            max_ref[head] = top
        parts = [
            jnp.exp2(scores[:, i : i + HEAD] * BASE2_SCALE - top).astype(jnp.bfloat16)
            for i in range(0, scores.shape[1], HEAD)
        ]
        return jnp.concatenate(parts, axis=1), factor

    def mix(head, n, weights, factor):
        total = matmul(weights, jnp.concatenate([blocks[n][2], ones], axis=1), NN)
        if not first:
            total = acc_ref[head] * jnp.concatenate([factor, factor], axis=1) + total
        if not last:
            acc_ref[head] = total
            return
        result = total[:, :HEAD] * (1.0 / total[:, HEAD:])
        position = lax.broadcasted_iota(jnp.int32, (ROWS, HEAD), 0)
        result = jnp.where(position < len_ref[0], result, 0.0)
        out_ref[:, head_lanes(head)] = result.astype(jnp.bfloat16)

    following = scores_of(*heads[0])
    for index, (head, n) in enumerate(heads):
        current = following
        if index + 1 < len(heads):
            following = scores_of(*heads[index + 1])
        mix(head, n, *weigh(head, current))


def kernel(
    q_hbm, ok_hbm, ov_hbm, len_hbm, pk_hbm, pv_hbm, out_ref,
    len_ref, q_ref, ok_ref, ov_ref, pk_ref, pv_ref, acc_ref, max_ref, part_ref, kv_ref,
    load_sems, part_send, part_recv, plane_send, plane_recv, core_send, core_recv,
):
    group, ctx = lax.axis_index("group"), lax.axis_index("ctx")
    x, z = group % 4, (group // 4) * 4 + ctx // 8
    y, core = (ctx // 2) % 4, ctx % 2

    def first_peer(a, j):
        return device(
            (x + RING_OFFSETS[a] * (1 - core)) % 4,
            (y + RING_OFFSETS[a] * core) % 4,
            (z + Z_OFFSETS[j]) % 8,
            core,
        )

    def last_peer(b):
        return device(
            (x + RING_OFFSETS[b] * core) % 4, (y + RING_OFFSETS[b] * (1 - core)) % 4, z, core
        )

    sibling = device(x, y, z, 1 - core)
    first_peers = {(a, j): first_peer(a, j) for j in range(PLANES) for a in range(RING) if a + j}
    last_peers = [last_peer(b) for b in range(RING)]

    barrier = pltpu.get_barrier_semaphore()
    for peer in list(first_peers.values()) + last_peers[1:] + [sibling]:
        pl.semaphore_signal(barrier, inc=1, device_id=peer, device_id_type=MESH)

    loads = [
        pltpu.make_async_copy(src, dst, load_sems.at[i])
        for i, (src, dst) in enumerate(
            [
                (pk_hbm, pk_ref), (pv_hbm, pv_ref), (len_hbm, len_ref),
                (ok_hbm, ok_ref), (ov_hbm, ov_ref), (q_hbm, q_ref),
            ]
        )
    ]
    for load in loads:
        load.start()
    loads[0].wait()
    loads[1].wait()
    for h in range(KV_HEADS):
        rows, lanes = slice(4 * h, 4 * h + 4), slice(HEAD * h, HEAD * h + HEAD)
        part_ref[0, 0, 0, rows] = pk_ref[:, lanes]
        part_ref[0, 0, 1, rows] = pv_ref[:, lanes]

    def remote(src, dst, send_sem, recv_sem, peer):
        return pltpu.make_async_remote_copy(
            src_ref=src, dst_ref=dst, send_sem=send_sem, recv_sem=recv_sem,
            device_id=peer, device_id_type=MESH,
        )

    def send_part():
        for j in range(PLANES):
            for a in range(RING):
                if a + j:
                    remote(
                        part_ref.at[0, 0], part_ref.at[j, a],
                        part_send.at[j], part_recv.at[j], first_peers[a, j],
                    ).start()

    def wait_part(j, sems):
        whole = part_ref.at[j] if j else part_ref.at[0, pl.ds(1, RING - 1)]
        pltpu.make_async_copy(whole, whole, sems.at[j]).wait()

    def send_plane(j):
        wait_part(j, part_recv)
        for i in range(2):
            for h in range(KV_HEADS):
                kv_ref[j, 0, 0, i, :, HEAD * h : HEAD * h + HEAD] = jnp.concatenate(
                    [part_ref[j, a, i, 4 * h : 4 * h + 4] for a in range(RING)], axis=0
                )
        for b in range(1, RING):
            remote(
                kv_ref.at[j, 0, 0], kv_ref.at[j, 0, b],
                plane_send.at[j], plane_recv.at[j], last_peers[b],
            ).start()

    def wait_plane(j, sems):
        whole = kv_ref.at[j, 0, pl.ds(1, RING - 1)]
        pltpu.make_async_copy(whole, whole, sems.at[j]).wait()

    def core_copy(j):
        return remote(kv_ref.at[j, 0], kv_ref.at[j, 1], core_send.at[j], core_recv.at[j], sibling)

    def share_plane(j):
        wait_plane(j, plane_recv)
        core_copy(j).start()

    refs = (len_ref, q_ref, out_ref, acc_ref, max_ref)

    def own(h, carry):
        lanes = head_lanes(h)
        attend([(h, ok_ref[:, lanes], ov_ref[:, lanes])], True, False, *refs)
        return carry

    pl.semaphore_wait(barrier, len(first_peers) + RING - 1 + 1)
    send_part()
    for load in loads[2:]:
        load.wait()
    lax.fori_loop(0, KV_HEADS - 1, own, 0)
    shared = 0
    for j in range(PLANES):
        if j == 1:
            lax.fori_loop(KV_HEADS - 1, KV_HEADS, own, 0)
        send_plane(j)
        if j >= 2 and j % 2 == 0 and shared < CHUNKS[0][1]:
            share_plane(shared)
            shared += 1
    for j in range(shared, CHUNKS[0][1]):
        share_plane(j)
    for index, (begin, end) in enumerate(CHUNKS):
        last = index + 1 == len(CHUNKS)
        coming = 0 if last else CHUNKS[index + 1][1] - end
        for j in range(begin, end):
            core_copy(j).wait_recv()

        width = LAST_HEADS if last else 1

        def prompt(step, carry, begin=begin, end=end, last=last, coming=coming, width=width):
            count = (end - begin) * 128
            blocks = []
            for n in range(width):
                h = step * width + n
                lanes = head_lanes(h)
                keys = kv_ref[begin:end, :, :, 0, :, lanes].reshape(count, HEAD)
                values = kv_ref[begin:end, :, :, 1, :, lanes].reshape(count, HEAD)
                blocks.append((h, keys, values))
            attend(blocks, False, last, *refs)
            if coming >= KV_HEADS:

                @pl.when(h == 1)
                def _():
                    share_plane(end)
                    share_plane(end + 1)

                @pl.when(h == 2)
                def _():
                    share_plane(end + 2)
                    share_plane(end + 3)
            elif coming:

                @pl.when(h < coming)
                def _():
                    share_plane(end + h)

            return carry

        lax.fori_loop(0, KV_HEADS // width, prompt, 0)
        for j in range(end + KV_HEADS, end + coming):
            share_plane(j)

    for j in range(PLANES):
        wait_part(j, part_send)
        wait_plane(j, plane_send)
        core_copy(j).wait_send()


def shards(queries, resp_keys, resp_values, lengths, prefix_keys, prefix_values):
    hbm = pl.BlockSpec(memory_space=pl.ANY)
    bf16, f32 = jnp.bfloat16, jnp.float32
    heads = KV_HEADS * GROUPS
    return pl.pallas_call(
        kernel,
        out_shape=pltpu.VMEM(queries.shape, bf16),
        in_specs=[hbm] * 6,
        out_specs=pl.BlockSpec(memory_space=pltpu.VMEM),
        scratch_shapes=[
            pltpu.SMEM(lengths.shape, jnp.int32),
            pltpu.VMEM(queries.shape, bf16),
            pltpu.VMEM(resp_keys.shape, bf16),
            pltpu.VMEM(resp_values.shape, bf16),
            pltpu.VMEM(prefix_keys.shape, bf16),
            pltpu.VMEM(prefix_values.shape, bf16),
            pltpu.VMEM((heads, ROWS, 2 * HEAD), f32),
            pltpu.VMEM((heads, ROWS, HEAD), f32),
            pltpu.VMEM((PLANES, RING, 2, 16, HEAD), bf16),
            pltpu.VMEM((PLANES, 2, RING, 2, 16, KV_HEADS * HEAD), bf16),
            pltpu.SemaphoreType.DMA((6,)),
        ]
        + [pltpu.SemaphoreType.DMA((PLANES,))] * 6,
        compiler_params=pltpu.CompilerParams(
            collective_id=0, has_side_effects=True, vmem_limit_bytes=58 << 20
        ),
        name="attend_and_gather",
    )(queries, resp_keys, resp_values, lengths, prefix_keys, prefix_values)


def solution(mesh):
    rows = P(("group", "ctx"), None)
    in_specs = (rows, rows, rows, P(("group", "ctx")), rows, rows)
    return jax.shard_map(shards, mesh=mesh, in_specs=in_specs, out_specs=rows, check_vma=False)
```
